256 devices in a mesh: head: 4 (over y), inner: 2 (over z_lo), outer: 32 (over z_hi, x, core).
Axes of the slice: x: 4, y: 4, z: 8 (z_hi: 4, z_lo: 2; z = z_hi * 2 + z_lo), core: 2. Of those that a mesh axis runs over, the one named last changes fastest.
Arguments:
- queries: bfloat16 [8192, 2048], P(('head', 'inner', 'outer')), may hold values from -2 to 2
- keys: bfloat16 [8192, 512], P(('head', 'inner', 'outer')), may hold values from -2 to 2
- values: bfloat16 [8192, 512], P(('head', 'inner', 'outer')), may hold values from -6 to 6
- out_grad: bfloat16 [8192, 2048], P(('head', 'inner', 'outer')), may hold values from -6 to 6
- span_order: int32 [256], replicated, may hold values from 0 to 255, each once
Outputs:
- query_grad: bfloat16 [8192, 2048], P(('head', 'inner', 'outer'))
- key_grad: bfloat16 [8192, 512], P(('head', 'inner', 'outer'))
- value_grad: bfloat16 [8192, 512], P(('head', 'inner', 'outer'))
The draws below stay inside these ranges and needn't reach their ends.
Inputs may be any that keep to these rules, and one draw needn't show every extreme that they name: span_order is a permutation of 0 to 255.
All inputs are finite; a program needn't handle non-finite values.
Results may differ from the reference program's by a relative error of at most 0.005.
Values may be sent and summed in bfloat16 or wider, within the bound.
A program may use at most 64 MiB of HBM per device.

```python
import math
import jax
import jax.numpy as jnp
from jax import lax

D_HEAD = 128
Q_HEADS = 16
KV_HEADS = 4
UNIT = 32
SEQ = 8192
DEVICES = 256


def steps_of(key, shape, pieces, low, largest):
    factor_of, own = 1.0, jax.random.fold_in(key, 6)
    for position, shards_of in pieces:
        draws = jnp.exp(jax.random.uniform(jax.random.fold_in(own, position), (shards_of,), jnp.float32, low / len(pieces), largest / len(pieces)))
        factor_of = factor_of * jnp.repeat(draws, shape[position] // shards_of).reshape([-1 if axis == position else 1 for axis in range(len(shape))])
    return factor_of


def gaussian(key, shape, deviation, limit, shards=(), kind=jnp.bfloat16):
    factor_of = steps_of(key, shape, shards, -0.22, 0.18) if shards else 1.0
    array = jax.random.normal(key, shape, jnp.float32) * deviation * factor_of
    return jnp.minimum(jnp.maximum(array, -limit), limit).astype(kind)


def setup_inputs(seed: int = 0) -> dict:
    key_of = jax.random.split(jax.random.key(seed), 6)
    queries = jnp.clip(jax.random.uniform(key_of[0], (SEQ, Q_HEADS * D_HEAD), jnp.float32, -2.0, 2.0) * steps_of(key_of[0], (SEQ, Q_HEADS * D_HEAD), ((0, 256),), -0.4, 0.0), -2.0, 2.0).astype(jnp.bfloat16)
    keys = jnp.clip(jax.random.uniform(key_of[1], (SEQ, KV_HEADS * D_HEAD), jnp.float32, -2.0, 2.0) * steps_of(key_of[1], (SEQ, KV_HEADS * D_HEAD), ((0, 256),), -0.4, 0.0), -2.0, 2.0).astype(jnp.bfloat16)
    values = gaussian(key_of[2], (SEQ, KV_HEADS * D_HEAD), 1.0, 6.0, ((0, 256),))
    out_grad = gaussian(key_of[3], (SEQ, Q_HEADS * D_HEAD), 1.0, 6.0, ((0, 256),))
    span_order = jax.random.permutation(key_of[4], DEVICES).astype(jnp.int32)
    return dict(queries=queries, keys=keys, values=values, out_grad=out_grad, span_order=span_order)


def reference(queries, keys, values, out_grad, span_order):
    group = Q_HEADS // KV_HEADS
    scale = 1.0 / math.sqrt(D_HEAD)
    tokens = jnp.arange(SEQ, dtype=jnp.int32)
    places = (span_order[tokens // UNIT] * UNIT + tokens % UNIT).astype(jnp.int32)
    q_block = math.gcd(SEQ, 512)
    blocks = SEQ // q_block

    def per_group(index):
        key_head = lax.dynamic_slice_in_dim(keys, index * D_HEAD, D_HEAD, 1).astype(jnp.float32)
        value_head = lax.dynamic_slice_in_dim(values, index * D_HEAD, D_HEAD, 1).astype(jnp.float32)
        query_heads = lax.dynamic_slice_in_dim(queries, index * group * D_HEAD, group * D_HEAD, 1)
        query_heads = query_heads.astype(jnp.float32).reshape(SEQ, group, D_HEAD)
        grad_heads = lax.dynamic_slice_in_dim(out_grad, index * group * D_HEAD, group * D_HEAD, 1)
        grad_heads = grad_heads.astype(jnp.float32).reshape(SEQ, group, D_HEAD)

        def step(carry, block):
            key_sum, value_sum = carry
            first = block * q_block
            query_rows = lax.dynamic_slice_in_dim(query_heads, first, q_block, 0)
            grad_rows = lax.dynamic_slice_in_dim(grad_heads, first, q_block, 0)
            query_places = lax.dynamic_slice_in_dim(places, first, q_block, 0)
            scores = jnp.einsum('igd,jd->gij', query_rows, key_head) * scale
            prob_grads = jnp.einsum('igd,jd->gij', grad_rows, value_head)
            allowed = places[None, None, :] <= query_places[None, :, None]
            raised = jnp.where(allowed, jnp.exp(scores), 0.0)
            norms = lax.optimization_barrier(jnp.sum(raised, axis=2))
            deltas = lax.optimization_barrier(jnp.sum(raised * prob_grads, axis=2)) / norms
            weights = raised / norms[:, :, None]
            probs = lax.optimization_barrier(weights.astype(jnp.bfloat16)).astype(jnp.float32)
            slopes = (weights * (prob_grads - deltas[:, :, None])).astype(jnp.bfloat16)
            slopes = lax.optimization_barrier(slopes).astype(jnp.float32)
            query_part = jnp.einsum('gij,jd->igd', slopes, key_head) * scale
            key_sum = key_sum + jnp.einsum('gij,igd->jd', slopes, query_rows)
            value_sum = value_sum + jnp.einsum('gij,igd->jd', probs, grad_rows)
            return ((key_sum, value_sum), query_part.astype(jnp.bfloat16))
        zeros = jnp.zeros((SEQ, D_HEAD), jnp.float32)
        sums, query_parts = lax.scan(step, (zeros, zeros), jnp.arange(blocks, dtype=jnp.int32))
        query_part = query_parts.reshape(SEQ, group * D_HEAD)
        return (query_part, (sums[0] * scale).astype(jnp.bfloat16), sums[1].astype(jnp.bfloat16))
    query_all, key_all, value_all = lax.map(per_group, jnp.arange(KV_HEADS, dtype=jnp.int32))
    query_grad = jnp.transpose(query_all, (1, 0, 2)).reshape(SEQ, Q_HEADS * D_HEAD)
    key_grad = jnp.transpose(key_all, (1, 0, 2)).reshape(SEQ, KV_HEADS * D_HEAD)
    value_grad = jnp.transpose(value_all, (1, 0, 2)).reshape(SEQ, KV_HEADS * D_HEAD)
    return (query_grad, key_grad, value_grad)
```

```python
import math

import jax
import jax.numpy as jnp
from jax import lax
from jax.experimental import pallas as pl
from jax.experimental.pallas import tpu as pltpu
from jax.sharding import PartitionSpec as P

MESH = pl.DeviceIdType.MESH
D = 128
G = 4
NY, NZ, NX, NC = 4, 8, 4, 2
U = 32
C = NY * U
QR = NX * C
KB = NC * C
GD = G * D
F32, BF16 = jnp.float32, jnp.bfloat16
SCALE = 1.0 / math.sqrt(D)
LOG2E = 1.4426950408889634
NT = (((1,), (1,)), ((), ()))
NN = (((1,), (0,)), ((), ()))


def dot(a, b, dims):
    return lax.dot_general(a, b, dims, preferred_element_type=F32)


def kernel(
    span, q_in, k_in, v_in, g_in, q_out, k_out, v_out,
    qg, kv, kt, es, ds, qp, nsum, wsum, stat, total, dqt, dkv, sib_in, z_out, z_in,
    dq_out, dq_in, q_fin, kv_fin,
    loc_sem, y_send, y_recv, x_send, x_recv, z_send, z_recv, c_send, c_recv,
    st_send, st_recv, dc_send, dc_recv, dz_send, dz_recv, dx_send, dx_recv, o_send, o_recv,
):
    y, zl, o = lax.axis_index("head"), lax.axis_index("inner"), lax.axis_index("outer")
    zh, x, c = o // (NX * NC), (o // NC) % NX, o % NC
    z = zh * 2 + zl

    def dev(y, z, x, c):
        return (y, z % 2, ((z // 2) * NX + x) * NC + c)

    def up(value, count, step):
        return (value + step + count) % count

    def copy(src, dst, send, recv, device):
        return pltpu.make_async_remote_copy(
            src_ref=src, dst_ref=dst, send_sem=send, recv_sem=recv, device_id=device, device_id_type=MESH
        )

    def y_dev(s):
        return dev(up(y, NY, s), z, x, c)

    def x_dev(s):
        return dev(y, z, up(x, NX, s), c)

    def z_dev(s):
        return dev(y, up(z, NZ, s), x, c)

    c_dev = dev(y, z, x, 1 - c)

    q_rows = pl.ds(pl.multiple_of(x * C + y * U, U), U)
    k_rows = pl.ds(pl.multiple_of((z * NC + c) * C + y * U, U), U)

    def pieces(to):
        wide = pl.ds(pl.multiple_of(to * GD, GD), GD)
        thin = pl.ds(pl.multiple_of(to * D, D), D)
        return (
            (q_in.at[:, wide], qg.at[q_rows, pl.ds(0, GD)]),
            (g_in.at[:, wide], qg.at[q_rows, pl.ds(GD, GD)]),
            (k_in.at[:, thin], kv.at[k_rows, pl.ds(0, D)]),
            (v_in.at[:, thin], kv.at[k_rows, pl.ds(D, D)]),
        )

    own = [pltpu.make_async_copy(a, b, loc_sem.at[i]) for i, (a, b) in enumerate(pieces(y))]
    for one in own:
        one.start()

    barrier = pltpu.get_barrier_semaphore()
    partners = (
        [y_dev(s) for s in range(1, NY)] + [x_dev(s) for s in range(1, NX)]
        + [z_dev(s) for s in range(1, NZ)] + [c_dev]
    )
    for device in partners:
        pl.semaphore_signal(barrier, inc=1, device_id=device, device_id_type=MESH)
    pl.semaphore_wait(barrier, len(partners))

    sends = []
    for s in range(1, NY):
        for i, (a, b) in enumerate(pieces(up(y, NY, s))):
            sends.append(copy(a, b, y_send.at[s - 1, i], y_recv.at[s - 1, i], y_dev(s)))
    for one in sends:
        one.start()

    lane = lax.broadcasted_iota(jnp.int32, (8, QR), 1)
    places = jnp.zeros((8, QR), jnp.int32)
    for xx in range(NX):
        for yy in range(NY):
            unit = yy * (NZ * NX * NC) + zl * (NZ // 2 * NX * NC) + (zh * NX + xx) * NC + c
            places = jnp.where(lane // U == xx * NY + yy, span[unit] * U, places)
    qp[...] = places + lane % U
    nsum[...] = jnp.zeros_like(nsum)
    wsum[...] = jnp.zeros_like(wsum)
    dqt[...] = jnp.zeros_like(dqt)

    for one in own:
        one.wait()
    for one in sends:
        one.wait_recv()

    def q_part(s, cols):
        return qg.at[pl.ds(pl.multiple_of(up(x, NX, s) * C, C), C), cols]

    def k_part(s, cols):
        return kv.at[pl.ds(pl.multiple_of((up(z, NZ, s) * NC + c) * C, C), C), cols]

    def q_copy(i, s, cols, to):
        part = q_part(s, cols)
        return copy(part, part, x_send.at[i], x_recv.at[i], x_dev(to))

    def k_copy(i, s, cols, to):
        part = k_part(s, cols)
        return copy(part, part, z_send.at[i], z_recv.at[i], z_dev(to))

    def c_copy(s):
        part = k_part(s, pl.ds(0, 2 * D))
        i = s % NZ
        return copy(part, part, c_send.at[i], c_recv.at[i], c_dev)

    every, low, high = pl.ds(0, 2 * GD), pl.ds(0, GD), pl.ds(GD, GD)
    k_every, k_low, k_high = pl.ds(0, 2 * D), pl.ds(0, D), pl.ds(D, D)
    qs = [q_copy(0, 0, every, 1), q_copy(1, 0, every, -1), q_copy(2, -1, low, 1), q_copy(3, 1, high, -1)]
    ks = []
    for s in range(4):
        a, b = (k_every, k_every) if s < 3 else (k_low, k_high)
        ks += [k_copy(2 * s, -s, a, 1), k_copy(2 * s + 1, s, b, -1)]
    cs = [c_copy(s) for s in (0, -1, 1, -2, 2, -3, 3, 4)]

    ks[0].start()
    ks[1].start()
    qs[0].start()
    qs[1].start()
    cs[0].start()
    for s in range(1, 4):
        ks[2 * s - 2].wait_recv()
        ks[2 * s].start()
        cs[2 * s - 1].start()
        ks[2 * s - 1].wait_recv()
        ks[2 * s + 1].start()
        cs[2 * s].start()
        if s == 2:
            qs[0].wait_recv()
            qs[2].start()
            qs[1].wait_recv()
            qs[3].start()
    ks[6].wait_recv()
    ks[7].wait_recv()
    cs[7].start()
    qs[2].wait_recv()
    qs[3].wait_recv()
    for one in cs:
        one.wait_recv()

    row = lax.broadcasted_iota(jnp.int32, (U, QR), 0)

    def first(b, carry):
        rows = pl.ds(pl.multiple_of(b * KB, KB), KB)
        keys, vals = kv[rows, 0:D], kv[rows, D : 2 * D]
        masks = []
        limit = qp[0:1, :]
        for cc in range(NC):
            for yy in range(NY):
                unit = yy * (NZ * NX * NC) + (b % 2) * (NZ // 2 * NX * NC) + ((b // 2) * NX + x) * NC + cc
                masks.append(row + span[unit] * U <= limit)
        mask = jnp.concatenate(masks, axis=0)
        kt[:, rows] = keys.T
        for h in range(G):
            cols = slice(h * QR, (h + 1) * QR)
            scores = dot(keys, qg[:, h * D : (h + 1) * D], NT)
            raised = jnp.where(mask, jnp.exp2(scores * (SCALE * LOG2E)), 0.0)
            grads = dot(vals, qg[:, GD + h * D : GD + (h + 1) * D], NT)
            es[rows, cols] = raised
            ds[rows, cols] = grads
            nsum[:, cols] += jnp.sum(raised.reshape(KB // 8, 8, QR), axis=0)
            wsum[:, cols] += jnp.sum((raised * grads).reshape(KB // 8, 8, QR), axis=0)
        return carry

    lax.fori_loop(0, NZ, first, 0)

    for h in range(G):
        cols = slice(h * QR, (h + 1) * QR)
        stat[x, h : h + 1, :] = jnp.sum(nsum[:, cols], axis=0, keepdims=True)
        stat[x, G + h : G + h + 1, :] = jnp.sum(wsum[:, cols], axis=0, keepdims=True)
    stats = [
        copy(stat.at[x], stat.at[x], st_send.at[s - 1], st_recv.at[s - 1], x_dev(s)) for s in range(1, NX)
    ]
    for one in stats:
        one.start()
    for one in stats:
        one.wait_recv()
    both = stat[0] + stat[1] + stat[2] + stat[3]
    inverse = 1.0 / both[0:G]
    total[0:G, :] = inverse
    total[G : 2 * G, :] = both[G : 2 * G] * inverse

    def block(t):
        return up(z, NZ, t + 1)

    def half(b, core):
        return pl.ds(pl.multiple_of(b * KB + core * C, C), C)

    def to_sibling(t):
        b = block(t)
        return copy(dkv.at[half(b, 1 - c), :], sib_in.at[b], dc_send.at[t], dc_recv.at[t], c_dev)

    def to_owner(t):
        b = block(t)
        return copy(z_out.at[b], z_in.at[z], dz_send.at[t], dz_recv.at[t], dev(y, b, x, c))

    def finish(t):
        b = block(t)
        to_sibling(t).wait_recv()
        z_out[b] = (dkv[half(b, c), :] + sib_in[b]).astype(BF16)
        to_owner(t).start()

    def second(t, carry):
        b = block(t)
        rows = pl.ds(pl.multiple_of(b * KB, KB), KB)
        key_sum = jnp.zeros((KB, D), F32)
        val_sum = jnp.zeros((KB, D), F32)
        for h in range(G):
            cols = slice(h * QR, (h + 1) * QR)
            weights = es[rows, cols] * total[h : h + 1, :]
            probs = weights.astype(BF16)
            slopes = (weights * (ds[rows, cols] - total[G + h : G + h + 1, :])).astype(BF16)
            val_sum += dot(probs, qg[:, GD + h * D : GD + (h + 1) * D], NN)
            key_sum += dot(slopes, qg[:, h * D : (h + 1) * D], NN)
            dqt[h] += dot(kt[:, rows], slopes, NN)
        dkv[rows, 0:D] = key_sum
        dkv[rows, D : 2 * D] = val_sum
        to_sibling(t).start()

        @pl.when(t > 0)
        def _():
            finish(t - 1)

        return carry

    lax.fori_loop(0, NZ, second, 0)

    for h in range(G):
        dq_out[:, h * D : (h + 1) * D] = (dqt[h].T * SCALE).astype(BF16)
    dxs = []
    for s in range(1, NX):
        part = dq_out.at[pl.ds(pl.multiple_of(up(x, NX, s) * C, C), C), :]
        dxs.append(copy(part, dq_in.at[x], dx_send.at[s - 1], dx_recv.at[s - 1], x_dev(s)))
    for one in dxs:
        one.start()
    to_sibling(NZ - 1).wait_recv()
    for one in dxs:
        one.wait_recv()
    q_sum = dq_out[pl.ds(pl.multiple_of(x * C, C), C), :].astype(F32)
    for s in range(1, NX):
        q_sum += dq_in[up(x, NX, s)].astype(F32)
    q_fin[...] = q_sum.astype(BF16)

    wide = pl.ds(pl.multiple_of(y * GD, GD), GD)
    thin = pl.ds(pl.multiple_of(y * D, D), D)

    def results(to):
        rows = pl.ds(pl.multiple_of(to * U, U), U)
        return (
            (q_fin.at[rows, :], q_out.at[:, wide]),
            (kv_fin.at[rows, pl.ds(0, D)], k_out.at[:, thin]),
            (kv_fin.at[rows, pl.ds(D, D)], v_out.at[:, thin]),
        )

    outs = []
    for s in range(1, NY):
        for i, (a, b) in enumerate(results(up(y, NY, s))):
            outs.append((i, copy(a, b, o_send.at[s - 1, i], o_recv.at[s - 1, i], y_dev(s))))
    mine = [(i, pltpu.make_async_copy(a, b, loc_sem.at[i])) for i, (a, b) in enumerate(results(y))]
    for i, one in outs + mine:
        if i == 0:
            one.start()

    for t in range(NZ - 1):
        to_owner(t).wait_recv()
    kv_sum = dkv[half(z, c), :] + sib_in[z]
    for s in range(1, NZ):
        kv_sum += z_in[up(z, NZ, s)].astype(F32)
    kv_fin[:, 0:D] = (kv_sum[:, 0:D] * SCALE).astype(BF16)
    kv_fin[:, D : 2 * D] = kv_sum[:, D : 2 * D].astype(BF16)
    for i, one in outs + mine:
        if i > 0:
            one.start()

    for one in sends + qs + ks + cs + stats + dxs:
        one.wait_send()
    for t in range(NZ):
        to_sibling(t).wait_send()
    for t in range(NZ - 1):
        to_owner(t).wait_send()
    for i, one in outs:
        one.wait()
    for i, one in mine:
        one.wait()


def body(queries, keys, values, out_grad, span_order):
    keys_all = NZ * NC * C
    dma = pltpu.SemaphoreType.DMA
    anywhere = pl.BlockSpec(memory_space=pl.ANY)
    return pl.pallas_call(
        kernel,
        out_shape=(
            jax.ShapeDtypeStruct(queries.shape, BF16),
            jax.ShapeDtypeStruct(keys.shape, BF16),
            jax.ShapeDtypeStruct(values.shape, BF16),
        ),
        in_specs=[pl.BlockSpec(memory_space=pltpu.SMEM)] + [anywhere] * 4,
        out_specs=(anywhere,) * 3,
        scratch_shapes=[
            pltpu.VMEM((QR, 2 * GD), BF16),
            pltpu.VMEM((keys_all, 2 * D), BF16),
            pltpu.VMEM((D, keys_all), BF16),
            pltpu.VMEM((keys_all, G * QR), F32),
            pltpu.VMEM((keys_all, G * QR), F32),
            pltpu.VMEM((8, QR), jnp.int32),
            pltpu.VMEM((8, G * QR), F32),
            pltpu.VMEM((8, G * QR), F32),
            pltpu.VMEM((NX, 2 * G, QR), F32),
            pltpu.VMEM((2 * G, QR), F32),
            pltpu.VMEM((G, D, QR), F32),
            pltpu.VMEM((keys_all, 2 * D), F32),
            pltpu.VMEM((NZ, C, 2 * D), F32),
            pltpu.VMEM((NZ, C, 2 * D), BF16),
            pltpu.VMEM((NZ, C, 2 * D), BF16),
            pltpu.VMEM((QR, GD), BF16),
            pltpu.VMEM((NX, C, GD), BF16),
            pltpu.VMEM((C, GD), BF16),
            pltpu.VMEM((C, 2 * D), BF16),
            dma((4,)),
            dma((NY - 1, 4)), dma((NY - 1, 4)),
            dma((4,)), dma((4,)),
            dma((8,)), dma((8,)),
            dma((NZ,)), dma((NZ,)),
            dma((NX - 1,)), dma((NX - 1,)),
            dma((NZ,)), dma((NZ,)),
            dma((NZ - 1,)), dma((NZ - 1,)),
            dma((NX - 1,)), dma((NX - 1,)),
            dma((NY - 1, 3)), dma((NY - 1, 3)),
        ],
        compiler_params=pltpu.CompilerParams(
            collective_id=0, has_side_effects=True, vmem_limit_bytes=56 * 2**20
        ),
    )(span_order, queries, keys, values, out_grad)


def solution(mesh):
    rows = P(("head", "inner", "outer"), None)
    return jax.shard_map(
        body,
        mesh=mesh,
        in_specs=(rows, rows, rows, rows, P()),
        out_specs=(rows, rows, rows),
        check_vma=False,
    )
```

```python
import math

import jax
import jax.numpy as jnp
from jax import lax
from jax.experimental import pallas as pl
from jax.experimental.pallas import tpu as pltpu
from jax.sharding import PartitionSpec as P

MESH = pl.DeviceIdType.MESH
D = 128
G = 4
NY, NZ, NX, NC = 4, 8, 4, 2
U = 32
C = NY * U
QR = NX * C
KB = NC * C
GD = G * D
F32, BF16 = jnp.float32, jnp.bfloat16
SCALE = 1.0 / math.sqrt(D)
LOG2E = 1.4426950408889634
NT = (((1,), (1,)), ((), ()))
NN = (((1,), (0,)), ((), ()))
REL = (0, 1, 3, 2)


def dot(a, b, dims):
    return lax.dot_general(a, b, dims, preferred_element_type=F32)


def kernel(
    span, q_in, k_in, v_in, g_in, q_out, k_out, v_out,
    qg, kv, kt, es, ds, qp, nsum, wsum, stat, stat_in, total, dqt, dkv, sib_in, z_out, z_in,
    dq_out, dq_in, q_fin, kv_fin,
    loc_sem, y_send, y_recv, x_send, x_recv, z_send, z_recv, c_send, c_recv,
    st_send, st_recv, dc_send, dc_recv, dz_send, dz_recv, dx_send, dx_recv, o_send, o_recv,
):
    y, zl, o = lax.axis_index("head"), lax.axis_index("inner"), lax.axis_index("outer")
    zh, x, c = o // (NX * NC), (o // NC) % NX, o % NC
    z = zh * 2 + zl

    def dev(y, z, x, c):
        return (y, z % 2, ((z // 2) * NX + x) * NC + c)

    def up(value, count, step):
        return (value + step + count) % count

    def copy(src, dst, send, recv, device):
        return pltpu.make_async_remote_copy(
            src_ref=src, dst_ref=dst, send_sem=send, recv_sem=recv, device_id=device, device_id_type=MESH
        )

    def y_dev(s):
        return dev(up(y, NY, s), z, x, c)

    def x_dev(s):
        return dev(y, z, up(x, NX, s), c)

    def z_dev(s):
        return dev(y, up(z, NZ, s), x, c)

    c_dev = dev(y, z, x, 1 - c)

    def away(p):
        return (p + 1) // 2 * (2 * (p % 2) - 1)

    def pieces(s):
        to, rows = up(y, NY, s), pl.ds((NY - s) % NY * U, U)
        wide = pl.ds(pl.multiple_of(to * GD, GD), GD)
        thin = pl.ds(pl.multiple_of(to * D, D), D)
        return (
            (k_in.at[:, thin], kv.at[rows, pl.ds(0, D)]),
            (v_in.at[:, thin], kv.at[rows, pl.ds(D, D)]),
            (q_in.at[:, wide], qg.at[rows, pl.ds(0, GD)]),
            (g_in.at[:, wide], qg.at[rows, pl.ds(GD, GD)]),
        )

    own = [pltpu.make_async_copy(a, b, loc_sem.at[i]) for i, (a, b) in enumerate(pieces(0))]
    for one in own:
        one.start()

    barrier = pltpu.get_barrier_semaphore()
    partners = (
        [y_dev(s) for s in range(1, NY)] + [x_dev(s) for s in range(1, NX)]
        + [z_dev(s) for s in range(1, NZ)] + [c_dev]
    )
    for device in partners:
        pl.semaphore_signal(barrier, inc=1, device_id=device, device_id_type=MESH)

    lane = lax.broadcasted_iota(jnp.int32, (8, QR), 1)
    places = jnp.zeros((8, QR), jnp.int32)
    for i in range(NX):
        for s in range(NY):
            unit = up(y, NY, s) * (NZ * NX * NC) + zl * (NZ // 2 * NX * NC) + (zh * NX + up(x, NX, REL[i])) * NC + c
            places = jnp.where(lane // U == i * NY + s, span[unit] * U, places)
    qp[...] = places + lane % U
    nsum[...] = jnp.zeros_like(nsum)
    wsum[...] = jnp.zeros_like(wsum)

    for one in own:
        one.wait()
    pl.semaphore_wait(barrier, len(partners))

    ys = {}
    for s in (1, 3, 2):
        for i, (a, b) in enumerate(pieces(s)):
            ys[s, i] = copy(a, b, y_send.at[s - 1, i], y_recv.at[s - 1, i], y_dev(s))
    def x_copy(way, s):
        rows = (NY - s) % NY * U
        slot, to, step, first, width = (
            (0, 2, 1, 0, 2 * GD), (0, 1, -1, 0, 2 * GD), (2, 3, 1, 0, GD), (1, 3, -1, GD, GD),
        )[way]
        return copy(
            qg.at[pl.ds(slot * C + rows, U), pl.ds(first, width)],
            qg.at[pl.ds(to * C + rows, U), pl.ds(first, width)],
            x_send.at[way, s], x_recv.at[way, s], x_dev(step),
        )

    def z_copy(i, slot, to, step, first, width):
        return copy(
            kv.at[pl.ds(slot * KB, C), pl.ds(first, width)],
            kv.at[pl.ds(to * KB, C), pl.ds(first, width)],
            z_send.at[i], z_recv.at[i], z_dev(step),
        )

    def c_copy(p):
        rows, there = p * KB, p * KB + C
        if not isinstance(p, int):
            rows, there = pl.multiple_of(rows, C), pl.multiple_of(there, C)
        return copy(kv.at[pl.ds(rows, C), :], kv.at[pl.ds(there, C), :], c_send.at[p], c_recv.at[p], c_dev)

    xs = {(way, s): x_copy(way, s) for way in range(4) for s in range(NY)}
    zs = {
        2: z_copy(2, 0, 2, 1, 0, 2 * D), 1: z_copy(1, 0, 1, -1, 0, 2 * D),
        4: z_copy(4, 0, 4, 2, 0, 2 * D), 3: z_copy(3, 0, 3, -2, 0, 2 * D),
        6: z_copy(6, 2, 6, 2, 0, 2 * D), 5: z_copy(5, 1, 5, -2, 0, 2 * D),
        7: z_copy(7, 4, 7, 2, 0, D), 8: z_copy(8, 3, 7, -2, D, D),
    }
    order = (0, 1, 3, 2)
    for i in range(2):
        for s in order[1:]:
            ys[s, i].start()
    xs[0, 0].start()
    xs[1, 0].start()
    for s in order[1:]:
        for i in (2, 3):
            ys[s, i].start()

    for s in order[1:]:
        ys[s, 0].wait_recv()
        ys[s, 1].wait_recv()
    for i in (2, 1, 4, 3):
        zs[i].start()
    c_copy(0).start()
    for s in order[1:]:
        ys[s, 2].wait_recv()
        ys[s, 3].wait_recv()
        xs[0, s].start()
        xs[1, s].start()
    for i in (2, 1):
        zs[i].wait_recv()
        zs[i + 4].start()
        c_copy(i).start()
    xs[0, 0].wait_recv()
    xs[2, 0].start()
    xs[1, 0].wait_recv()
    xs[3, 0].start()
    zs[4].wait_recv()
    zs[7].start()
    c_copy(4).start()
    zs[3].wait_recv()
    zs[8].start()
    c_copy(3).start()
    for s in order[1:]:
        xs[0, s].wait_recv()
        xs[2, s].start()
        xs[1, s].wait_recv()
        xs[3, s].start()
    for i in (6, 5):
        zs[i].wait_recv()
        c_copy(i).start()

    row = lax.broadcasted_iota(jnp.int32, (U, 1), 0)

    def tile(p, low, width):
        rows = pl.ds(p * KB if isinstance(p, int) else pl.multiple_of(p * KB, KB), KB)
        keys, vals = kv[rows, 0:D], kv[rows, D : 2 * D]
        masks = []
        limit = jnp.broadcast_to(qp[0:1, low : low + width], (U, width))
        zz = up(z, NZ, away(p))
        for cc in (c, 1 - c):
            for s in range(NY):
                unit = up(y, NY, s) * (NZ * NX * NC) + (zz % 2) * (NZ // 2 * NX * NC) + ((zz // 2) * NX + x) * NC + cc
                masks.append(row + span[unit] * U <= limit)
        mask = jnp.concatenate(masks, axis=0)
        if low == 0:
            kt[:, rows] = keys.T
        for h in range(G):
            cols = slice(h * QR + low, h * QR + low + width)
            scores = dot(keys, qg[low : low + width, h * D : (h + 1) * D], NT)
            raised = jnp.where(mask, jnp.exp2(scores * (SCALE * LOG2E)), 0.0)
            grads = dot(vals, qg[low : low + width, GD + h * D : GD + (h + 1) * D], NT)
            es[rows, cols] = raised
            ds[rows, cols] = grads
            nsum[:, cols] += jnp.sum(raised.reshape(KB // 8, 8, width), axis=0)
            wsum[:, cols] += jnp.sum((raised * grads).reshape(KB // 8, 8, width), axis=0)

    def near(p, carry):
        @pl.when(p > 0)
        def _():
            c_copy(p).wait_recv()

        tile(p, 0, QR // 2)
        return carry

    def far(p, carry):
        tile(p, QR // 2, QR // 2)
        return carry

    c_copy(0).wait_recv()
    lax.fori_loop(0, NZ - 1, near, 0)
    zs[7].wait_recv()
    zs[8].wait_recv()
    c_copy(7).start()
    for s in range(NY):
        xs[2, s].wait_recv()
        xs[3, s].wait_recv()
    lax.fori_loop(0, NZ - 1, far, 0)
    c_copy(7).wait_recv()
    tile(7, 0, QR)

    for h in range(G):
        cols = slice(h * QR, (h + 1) * QR)
        stat[h : h + 1, :] = jnp.sum(nsum[:, cols], axis=0, keepdims=True)
        stat[G + h : G + h + 1, :] = jnp.sum(wsum[:, cols], axis=0, keepdims=True)
    stats = [
        copy(stat, stat_in.at[s - 1], st_send.at[s - 1], st_recv.at[s - 1], x_dev(s)) for s in range(1, NX)
    ]
    for one in stats:
        one.start()
    dqt[...] = jnp.zeros_like(dqt)
    for one in stats:
        one.wait_recv()
    for i in range(NX):
        both = stat[:, i * C : (i + 1) * C]
        for s in range(1, NX):
            j = REL.index((REL[i] + s) % NX)
            both += stat_in[s - 1, :, j * C : (j + 1) * C]
        inverse = 1.0 / both[0:G]
        total[0:G, i * C : (i + 1) * C] = inverse
        total[G : 2 * G, i * C : (i + 1) * C] = both[G : 2 * G] * inverse

    def half(p, core):
        return pl.ds(pl.multiple_of(p * KB + core * C, C), C)

    def to_sibling(p):
        return copy(dkv.at[half(p, 1), :], sib_in.at[p], dc_send.at[p], dc_recv.at[p], c_dev)

    def to_owner(p):
        return copy(z_out.at[p], z_in.at[p], dz_send.at[p], dz_recv.at[p], z_dev(away(p)))

    def finish(p):
        to_sibling(p).wait_recv()
        z_out[p] = (dkv[half(p, 0), :] + sib_in[p]).astype(BF16)
        to_owner(p).start()

    def second(t, carry):
        p = NZ - 1 - t
        rows = pl.ds(pl.multiple_of(p * KB, KB), KB)
        key_sum = jnp.zeros((KB, D), F32)
        val_sum = jnp.zeros((KB, D), F32)
        for h in range(G):
            cols = slice(h * QR, (h + 1) * QR)
            weights = es[rows, cols] * total[h : h + 1, :]
            probs = weights.astype(BF16)
            slopes = (weights * (ds[rows, cols] - total[G + h : G + h + 1, :])).astype(BF16)
            val_sum += dot(probs, qg[:, GD + h * D : GD + (h + 1) * D], NN)
            key_sum += dot(slopes, qg[:, h * D : (h + 1) * D], NN)
            dqt[h] += dot(kt[:, rows], slopes, NN)
        dkv[rows, 0:D] = key_sum
        dkv[rows, D : 2 * D] = val_sum
        to_sibling(p).start()

        @pl.when(t > 0)
        def _():
            finish(p + 1)

        return carry

    lax.fori_loop(0, NZ, second, 0)

    for h in range(G):
        dq_out[:, h * D : (h + 1) * D] = (dqt[h].T * SCALE).astype(BF16)
    dxs = []
    for s in range(1, NX):
        part = dq_out.at[pl.ds(REL.index(s) * C, C), :]
        dxs.append(copy(part, dq_in.at[s - 1], dx_send.at[s - 1], dx_recv.at[s - 1], x_dev(s)))
    for one in dxs:
        one.start()
    for one in dxs:
        one.wait_recv()
    q_sum = dq_out[0:C, :].astype(F32)
    for s in range(1, NX):
        q_sum += dq_in[s - 1].astype(F32)
    q_fin[...] = q_sum.astype(BF16)

    wide = pl.ds(pl.multiple_of(y * GD, GD), GD)
    thin = pl.ds(pl.multiple_of(y * D, D), D)

    def results(s):
        rows = pl.ds(s * U, U)
        return (
            (q_fin.at[rows, :], q_out.at[:, wide]),
            (kv_fin.at[rows, pl.ds(0, D)], k_out.at[:, thin]),
            (kv_fin.at[rows, pl.ds(D, D)], v_out.at[:, thin]),
        )

    outs = []
    for s in range(1, NY):
        for i, (a, b) in enumerate(results(s)):
            outs.append((i, copy(a, b, o_send.at[s - 1, i], o_recv.at[s - 1, i], y_dev(s))))
    mine = [(i, pltpu.make_async_copy(a, b, loc_sem.at[i])) for i, (a, b) in enumerate(results(0))]
    for i, one in outs + mine:
        if i == 0:
            one.start()

    to_sibling(0).wait_recv()
    kv_sum = dkv[0:C, :] + sib_in[0]
    for p in range(NZ - 1, 0, -1):
        to_owner(p).wait_recv()
        kv_sum += z_in[p].astype(F32)
    kv_fin[:, 0:D] = (kv_sum[:, 0:D] * SCALE).astype(BF16)
    kv_fin[:, D : 2 * D] = kv_sum[:, D : 2 * D].astype(BF16)
    for i, one in outs + mine:
        if i > 0:
            one.start()

    for one in [*ys.values(), *xs.values(), *zs.values(), *stats, *dxs]:
        one.wait_send()
    for p in range(NZ):
        c_copy(p).wait_send()
        to_sibling(p).wait_send()
        if p > 0:
            to_owner(p).wait_send()
    for i, one in outs:
        one.wait()
    for i, one in mine:
        one.wait()


def body(queries, keys, values, out_grad, span_order):
    keys_all = NZ * NC * C
    dma = pltpu.SemaphoreType.DMA
    anywhere = pl.BlockSpec(memory_space=pl.ANY)
    return pl.pallas_call(
        kernel,
        out_shape=(
            jax.ShapeDtypeStruct(queries.shape, BF16),
            jax.ShapeDtypeStruct(keys.shape, BF16),
            jax.ShapeDtypeStruct(values.shape, BF16),
        ),
        in_specs=[pl.BlockSpec(memory_space=pltpu.SMEM)] + [anywhere] * 4,
        out_specs=(anywhere,) * 3,
        scratch_shapes=[
            pltpu.VMEM((QR, 2 * GD), BF16),
            pltpu.VMEM((keys_all, 2 * D), BF16),
            pltpu.VMEM((D, keys_all), BF16),
            pltpu.VMEM((keys_all, G * QR), F32),
            pltpu.VMEM((keys_all, G * QR), F32),
            pltpu.VMEM((8, QR), jnp.int32),
            pltpu.VMEM((8, G * QR), F32),
            pltpu.VMEM((8, G * QR), F32),
            pltpu.VMEM((2 * G, QR), F32),
            pltpu.VMEM((NX - 1, 2 * G, QR), F32),
            pltpu.VMEM((2 * G, QR), F32),
            pltpu.VMEM((G, D, QR), F32),
            pltpu.VMEM((keys_all, 2 * D), F32),
            pltpu.VMEM((NZ, C, 2 * D), F32),
            pltpu.VMEM((NZ, C, 2 * D), BF16),
            pltpu.VMEM((NZ, C, 2 * D), BF16),
            pltpu.VMEM((QR, GD), BF16),
            pltpu.VMEM((NX - 1, C, GD), BF16),
            pltpu.VMEM((C, GD), BF16),
            pltpu.VMEM((C, 2 * D), BF16),
            dma((4,)),
            dma((NY - 1, 4)), dma((NY - 1, 4)),
            dma((4, NY)), dma((4, NY)),
            dma((NZ + 1,)), dma((NZ + 1,)),
            dma((NZ,)), dma((NZ,)),
            dma((NX - 1,)), dma((NX - 1,)),
            dma((NZ,)), dma((NZ,)),
            dma((NZ,)), dma((NZ,)),
            dma((NX - 1,)), dma((NX - 1,)),
            dma((NY - 1, 3)), dma((NY - 1, 3)),
        ],
        compiler_params=pltpu.CompilerParams(
            collective_id=0, has_side_effects=True, vmem_limit_bytes=56 * 2**20
        ),
    )(span_order, queries, keys, values, out_grad)


def solution(mesh):
    rows = P(("head", "inner", "outer"), None)
    return jax.shard_map(
        body,
        mesh=mesh,
        in_specs=(rows, rows, rows, rows, P()),
        out_specs=(rows, rows, rows),
        check_vma=False,
    )
```

```python
import math

import jax
import jax.numpy as jnp
from jax import lax
from jax.experimental import pallas as pl
from jax.experimental.pallas import tpu as pltpu
from jax.sharding import PartitionSpec as P

MESH = pl.DeviceIdType.MESH
D = 128
G = 4
NY, NZ, NX, NC = 4, 8, 4, 2
U = 32
C = NY * U
QR = NX * C
KB = NC * C
GD = G * D
F32, BF16 = jnp.float32, jnp.bfloat16
SCALE = 1.0 / math.sqrt(D)
LOG2E = 1.4426950408889634
NT = (((1,), (1,)), ((), ()))
NN = (((1,), (0,)), ((), ()))
REL = (0, 1, 3, 2)


def dot(a, b, dims):
    return lax.dot_general(a, b, dims, preferred_element_type=F32)


def kernel(
    span, q_in, k_in, v_in, g_in, q_parts, kv_parts,
    qg, kv, kt, es, ds, qp, nsum, wsum, stat, stat_in, total, dqt, dkv, sib_in, z_out, z_in,
    dq_out, dq_in, q_fin, kv_fin,
    loc_sem, y_send, y_recv, x_send, x_recv, z_send, z_recv, c_send, c_recv,
    st_send, st_recv, dc_send, dc_recv, dz_send, dz_recv, dx_send, dx_recv, o_send, o_recv,
):
    y, zl, o = lax.axis_index("head"), lax.axis_index("inner"), lax.axis_index("outer")
    zh, x, c = o // (NX * NC), (o // NC) % NX, o % NC
    z = zh * 2 + zl

    def dev(y, z, x, c):
        return (y, z % 2, ((z // 2) * NX + x) * NC + c)

    def up(value, count, step):
        return (value + step + count) % count

    def copy(src, dst, send, recv, device):
        return pltpu.make_async_remote_copy(
            src_ref=src, dst_ref=dst, send_sem=send, recv_sem=recv, device_id=device, device_id_type=MESH
        )

    def y_dev(s):
        return dev(up(y, NY, s), z, x, c)

    def x_dev(s):
        return dev(y, z, up(x, NX, s), c)

    def z_dev(s):
        return dev(y, up(z, NZ, s), x, c)

    c_dev = dev(y, z, x, 1 - c)

    def away(p):
        return (p + 1) // 2 * (2 * (p % 2) - 1)

    def pieces(s):
        to, rows = up(y, NY, s), pl.ds((NY - s) % NY * U, U)
        wide = pl.ds(pl.multiple_of(to * GD, GD), GD)
        thin = pl.ds(pl.multiple_of(to * D, D), D)
        return (
            (k_in.at[:, thin], kv.at[rows, pl.ds(0, D)]),
            (v_in.at[:, thin], kv.at[rows, pl.ds(D, D)]),
            (q_in.at[:, wide], qg.at[rows, pl.ds(0, GD)]),
            (g_in.at[:, wide], qg.at[rows, pl.ds(GD, GD)]),
        )

    own = [pltpu.make_async_copy(a, b, loc_sem.at[i]) for i, (a, b) in enumerate(pieces(0))]
    for one in own:
        one.start()

    barrier = pltpu.get_barrier_semaphore()
    partners = (
        [y_dev(s) for s in range(1, NY)] + [x_dev(s) for s in range(1, NX)]
        + [z_dev(s) for s in (1, -1, 2, -2)] + [c_dev]
    )
    for device in partners:
        pl.semaphore_signal(barrier, inc=1, device_id=device, device_id_type=MESH)

    lane = lax.broadcasted_iota(jnp.int32, (8, QR), 1)
    places = jnp.zeros((8, QR), jnp.int32)
    for i in range(NX):
        for s in range(NY):
            unit = up(y, NY, s) * (NZ * NX * NC) + zl * (NZ // 2 * NX * NC) + (zh * NX + up(x, NX, REL[i])) * NC + c
            places = jnp.where(lane // U == i * NY + s, span[unit] * U, places)
    qp[...] = places + lane % U
    nsum[...] = jnp.zeros_like(nsum)
    wsum[...] = jnp.zeros_like(wsum)

    for one in own:
        one.wait()
    pl.semaphore_wait(barrier, len(partners))

    ys = {}
    for s in (1, 3, 2):
        for i, (a, b) in enumerate(pieces(s)):
            ys[s, i] = copy(a, b, y_send.at[s - 1, i], y_recv.at[s - 1, i], y_dev(s))
    def x_copy(way, s):
        rows = (NY - s) % NY * U
        slot, to, step, first, width = (
            (0, 2, 1, 0, 2 * GD), (0, 1, -1, 0, 2 * GD), (2, 3, 1, 0, GD), (1, 3, -1, GD, GD),
        )[way]
        return copy(
            qg.at[pl.ds(slot * C + rows, U), pl.ds(first, width)],
            qg.at[pl.ds(to * C + rows, U), pl.ds(first, width)],
            x_send.at[way, s], x_recv.at[way, s], x_dev(step),
        )

    def z_copy(i, slot, to, step, first, width):
        return copy(
            kv.at[pl.ds(slot * KB, C), pl.ds(first, width)],
            kv.at[pl.ds(to * KB, C), pl.ds(first, width)],
            z_send.at[i], z_recv.at[i], z_dev(step),
        )

    def c_copy(p):
        rows, there = p * KB, p * KB + C
        if not isinstance(p, int):
            rows, there = pl.multiple_of(rows, C), pl.multiple_of(there, C)
        return copy(kv.at[pl.ds(rows, C), :], kv.at[pl.ds(there, C), :], c_send.at[p], c_recv.at[p], c_dev)

    xs = {(way, s): x_copy(way, s) for way in range(4) for s in range(NY)}
    zs = {
        2: z_copy(2, 0, 2, 1, 0, 2 * D), 1: z_copy(1, 0, 1, -1, 0, 2 * D),
        4: z_copy(4, 0, 4, 2, 0, 2 * D), 3: z_copy(3, 0, 3, -2, 0, 2 * D),
        6: z_copy(6, 2, 6, 2, 0, 2 * D), 5: z_copy(5, 1, 5, -2, 0, 2 * D),
        7: z_copy(7, 4, 7, 2, 0, D), 8: z_copy(8, 3, 7, -2, D, D),
    }
    order = (0, 1, 3, 2)
    for i in range(2):
        for s in order[1:]:
            ys[s, i].start()
    xs[0, 0].start()
    xs[1, 0].start()
    for s in order[1:]:
        for i in (2, 3):
            ys[s, i].start()

    for s in order[1:]:
        ys[s, 0].wait_recv()
        ys[s, 1].wait_recv()
    for i in (2, 1, 4, 3):
        zs[i].start()
    c_copy(0).start()
    for s in order[1:]:
        ys[s, 2].wait_recv()
        ys[s, 3].wait_recv()
        xs[0, s].start()
        xs[1, s].start()
    for i in (2, 1):
        zs[i].wait_recv()
        zs[i + 4].start()
        c_copy(i).start()
    xs[0, 0].wait_recv()
    xs[2, 0].start()
    xs[1, 0].wait_recv()
    xs[3, 0].start()
    zs[4].wait_recv()
    zs[7].start()
    c_copy(4).start()
    zs[3].wait_recv()
    zs[8].start()
    c_copy(3).start()
    for s in order[1:]:
        xs[0, s].wait_recv()
        xs[2, s].start()
        xs[1, s].wait_recv()
        xs[3, s].start()

    row = lax.broadcasted_iota(jnp.int32, (U, 1), 0)

    def tile(p, low, width):
        rows = pl.ds(p * KB if isinstance(p, int) else pl.multiple_of(p * KB, KB), KB)
        keys, vals = kv[rows, 0:D], kv[rows, D : 2 * D]
        masks = []
        limit = jnp.broadcast_to(qp[0:1, low : low + width], (U, width))
        zz = up(z, NZ, away(p))
        for cc in (c, 1 - c):
            for s in range(NY):
                unit = up(y, NY, s) * (NZ * NX * NC) + (zz % 2) * (NZ // 2 * NX * NC) + ((zz // 2) * NX + x) * NC + cc
                masks.append(row + span[unit] * U <= limit)
        mask = jnp.concatenate(masks, axis=0)
        for h in range(G):
            cols = slice(h * QR + low, h * QR + low + width)
            scores = dot(keys, qg[low : low + width, h * D : (h + 1) * D], NT)
            raised = jnp.where(mask, jnp.exp2(scores * (SCALE * LOG2E)), 0.0)
            grads = dot(vals, qg[low : low + width, GD + h * D : GD + (h + 1) * D], NT)
            es[rows, cols] = raised
            ds[rows, cols] = grads
            nsum[:, cols] += jnp.sum(raised.reshape(KB // 8, 8, width), axis=0)
            wsum[:, cols] += jnp.sum((raised * grads).reshape(KB // 8, 8, width), axis=0)

    def near(p, carry):
        @pl.when(p == 2)
        def _():
            for i in (6, 5):
                zs[i].wait_recv()
                c_copy(i).start()

        @pl.when(p > 0)
        def _():
            c_copy(p).wait_recv()

        tile(p, 0, QR // 2)
        return carry

    def far(p, carry):
        @pl.when(p == 1)
        def _():
            zs[7].wait_recv()
            zs[8].wait_recv()
            c_copy(7).start()

        tile(p, QR // 2, QR // 2)
        return carry

    c_copy(0).wait_recv()
    lax.fori_loop(0, NZ - 1, near, 0)
    for s in range(NY):
        xs[2, s].wait_recv()
        xs[3, s].wait_recv()
    lax.fori_loop(0, NZ - 1, far, 0)
    c_copy(7).wait_recv()
    tile(7, 0, QR)

    for h in range(G):
        cols = slice(h * QR, (h + 1) * QR)
        stat[h : h + 1, :] = jnp.sum(nsum[:, cols], axis=0, keepdims=True)
        stat[G + h : G + h + 1, :] = jnp.sum(wsum[:, cols], axis=0, keepdims=True)
    stats = [
        copy(stat, stat_in.at[s - 1], st_send.at[s - 1], st_recv.at[s - 1], x_dev(s)) for s in range(1, NX)
    ]
    for one in stats:
        one.start()
    dqt[...] = jnp.zeros_like(dqt)
    for p in range(NZ):
        kt[:, p * KB : (p + 1) * KB] = kv[p * KB : (p + 1) * KB, 0:D].T
    for one in stats:
        one.wait_recv()
    for i in range(NX):
        both = stat[:, i * C : (i + 1) * C]
        for s in range(1, NX):
            j = REL.index((REL[i] + s) % NX)
            both += stat_in[s - 1, :, j * C : (j + 1) * C]
        inverse = 1.0 / both[0:G]
        total[0:G, i * C : (i + 1) * C] = inverse
        total[G : 2 * G, i * C : (i + 1) * C] = both[G : 2 * G] * inverse

    def half(p, core):
        return pl.ds(pl.multiple_of(p * KB + core * C, C), C)

    def to_sibling(p):
        return copy(dkv.at[half(p, 1), :], sib_in.at[p], dc_send.at[p], dc_recv.at[p], c_dev)

    def z_sum(i, p, step, first, width):
        cols = pl.ds(first, width)
        return copy(z_out.at[p, :, cols], z_in.at[p, :, cols], dz_send.at[i], dz_recv.at[i], z_dev(step))

    zsums = {
        7: z_sum(7, 7, 2, 0, D), 8: z_sum(8, 7, -2, D, D),
        6: z_sum(6, 6, -1, 0, 2 * D), 5: z_sum(5, 5, 1, 0, 2 * D),
        4: z_sum(4, 4, -2, 0, 2 * D), 3: z_sum(3, 3, 2, 0, 2 * D),
        2: z_sum(2, 2, -1, 0, 2 * D), 1: z_sum(1, 1, 1, 0, 2 * D),
    }

    def finish(p):
        to_sibling(p).wait_recv()
        z_out[p] = (dkv[half(p, 0), :] + sib_in[p]).astype(BF16)

    def relay(p, nearer, part, first):
        to_sibling(p).wait_recv()
        zsums[nearer].wait_recv()
        zsums[part].wait_recv()
        both = dkv[half(p, 0), :] + sib_in[p] + z_in[nearer].astype(F32)
        cols, rest = slice(first, first + D), slice(D - first, 2 * D - first)
        z_out[p, :, cols] = (both[:, cols] + z_in[7, :, cols].astype(F32)).astype(BF16)
        z_out[p, :, rest] = both[:, rest].astype(BF16)
        zsums[p].start()

    def sums(p, heads, rows):
        key_sum = jnp.zeros((KB, D), F32)
        val_sum = jnp.zeros((KB, D), F32)
        for h in heads:
            cols = slice(h * QR, (h + 1) * QR)
            weights = es[rows, cols] * total[h : h + 1, :]
            probs = weights.astype(BF16)
            slopes = (weights * (ds[rows, cols] - total[G + h : G + h + 1, :])).astype(BF16)
            val_sum += dot(probs, qg[:, GD + h * D : GD + (h + 1) * D], NN)
            key_sum += dot(slopes, qg[:, h * D : (h + 1) * D], NN)
            dqt[h] += dot(kt[:, rows], slopes, NN)
        return key_sum, val_sum

    def block(p):
        return pl.ds(pl.multiple_of(p * KB, KB), KB)

    def second(t, carry):
        p = NZ - 1 - t
        rows = block(p)
        dkv[rows, 0:D], dkv[rows, D : 2 * D] = sums(p, range(0, G // 2), rows)
        return carry

    def third(t, carry):
        p = NZ - 1 - t
        rows = block(p)
        key_sum, val_sum = sums(p, range(G // 2, G), rows)
        dkv[rows, 0:D] += key_sum
        dkv[rows, D : 2 * D] += val_sum
        to_sibling(p).start()

        @pl.when((p == 5) | (p == 4) | (p == 3) | (p == 0))
        def _():
            finish(p + 2)

        @pl.when(p == 5)
        def _():
            zsums[7].start()
            zsums[8].start()

        for q in (6, 5, 2):

            @pl.when(p == q - 2)
            def _(q=q):
                zsums[q].start()

        return carry

    def q_sums(half):
        cols = pl.ds(half * GD // 2, GD // 2)
        for h in range(half * G // 2, (half + 1) * G // 2):
            dq_out[:, h * D : (h + 1) * D] = (dqt[h].T * SCALE).astype(BF16)
        copies = []
        for s in (2, 1, 3):
            part = dq_out.at[pl.ds(REL.index(s) * C, C), cols]
            i = half * NX + s
            copies.append(copy(part, dq_in.at[s - 1, :, cols], dx_send.at[i], dx_recv.at[i], x_dev(s)))
        for one in copies:
            one.start()
        return copies

    def to_tokens(i, src, dst):
        copies = [pltpu.make_async_copy(src.at[pl.ds(0, U), :], dst, loc_sem.at[i])]
        for s in range(1, NY):
            copies.append(copy(src.at[pl.ds(s * U, U), :], dst, o_send.at[i, s], o_recv.at[i, s], y_dev(s)))
        for one in copies:
            one.start()
        return copies

    def q_done(half, copies):
        cols = slice(half * GD // 2, (half + 1) * GD // 2)
        for one in copies:
            one.wait_recv()
        q_sum = dq_out[0:C, cols].astype(F32)
        for s in range(1, NX):
            q_sum += dq_in[s - 1, :, cols].astype(F32)
        q_fin[half] = q_sum.astype(BF16)
        return to_tokens(half, q_fin.at[half], q_parts.at[y, half])

    lax.fori_loop(0, NZ, second, 0)
    low_sums = q_sums(0)
    lax.fori_loop(0, NZ, third, 0)
    high_sums = q_sums(1)
    finish(1)
    zsums[1].start()
    relay(4, 6, 8, D)
    relay(3, 5, 7, 0)
    outs = q_done(0, low_sums)
    to_sibling(0).wait_recv()
    kv_sum = dkv[0:C, :] + sib_in[0]
    for p in (1, 2):
        zsums[p].wait_recv()
        kv_sum += z_in[p].astype(F32)
    outs += q_done(1, high_sums)
    for p in (3, 4):
        zsums[p].wait_recv()
        kv_sum += z_in[p].astype(F32)
    kv_fin[:, 0:D] = (kv_sum[:, 0:D] * SCALE).astype(BF16)
    kv_fin[:, D : 2 * D] = kv_sum[:, D : 2 * D].astype(BF16)
    outs += to_tokens(2, kv_fin, kv_parts.at[y])

    for one in [*ys.values(), *xs.values(), *zs.values(), *zsums.values(), *stats, *low_sums, *high_sums]:
        one.wait_send()
    for p in range(NZ):
        c_copy(p).wait_send()
        to_sibling(p).wait_send()
    for one in outs:
        one.wait()


def last_columns(q_parts, kv_parts, q_out, k_out, v_out):
    for h in range(NY):
        for half in range(2):
            first = h * GD + half * GD // 2
            q_out[:, first : first + GD // 2] = q_parts[h, half]
        k_out[:, h * D : (h + 1) * D] = kv_parts[h, :, 0:D]
        v_out[:, h * D : (h + 1) * D] = kv_parts[h, :, D : 2 * D]


def body(queries, keys, values, out_grad, span_order):
    keys_all = NZ * NC * C
    dma = pltpu.SemaphoreType.DMA
    anywhere = pl.BlockSpec(memory_space=pl.ANY)
    parts = pl.pallas_call(
        kernel,
        out_shape=(
            jax.ShapeDtypeStruct((NY, 2, U, GD // 2), BF16),
            jax.ShapeDtypeStruct((NY, U, 2 * D), BF16),
        ),
        in_specs=[pl.BlockSpec(memory_space=pltpu.SMEM)] + [anywhere] * 4,
        out_specs=(anywhere,) * 2,
        scratch_shapes=[
            pltpu.VMEM((QR, 2 * GD), BF16),
            pltpu.VMEM((keys_all, 2 * D), BF16),
            pltpu.VMEM((D, keys_all), BF16),
            pltpu.VMEM((keys_all, G * QR), F32),
            pltpu.VMEM((keys_all, G * QR), F32),
            pltpu.VMEM((8, QR), jnp.int32),
            pltpu.VMEM((8, G * QR), F32),
            pltpu.VMEM((8, G * QR), F32),
            pltpu.VMEM((2 * G, QR), F32),
            pltpu.VMEM((NX - 1, 2 * G, QR), F32),
            pltpu.VMEM((2 * G, QR), F32),
            pltpu.VMEM((G, D, QR), F32),
            pltpu.VMEM((keys_all, 2 * D), F32),
            pltpu.VMEM((NZ, C, 2 * D), F32),
            pltpu.VMEM((NZ, C, 2 * D), BF16),
            pltpu.VMEM((NZ, C, 2 * D), BF16),
            pltpu.VMEM((QR, GD), BF16),
            pltpu.VMEM((NX - 1, C, GD), BF16),
            pltpu.VMEM((2, C, GD // 2), BF16),
            pltpu.VMEM((C, 2 * D), BF16),
            dma((4,)),
            dma((NY - 1, 4)), dma((NY - 1, 4)),
            dma((4, NY)), dma((4, NY)),
            dma((NZ + 1,)), dma((NZ + 1,)),
            dma((NZ,)), dma((NZ,)),
            dma((NX - 1,)), dma((NX - 1,)),
            dma((NZ,)), dma((NZ,)),
            dma((NZ + 1,)), dma((NZ + 1,)),
            dma((2 * NX,)), dma((2 * NX,)),
            dma((3, NY)), dma((3, NY)),
        ],
        compiler_params=pltpu.CompilerParams(
            collective_id=0, has_side_effects=True, vmem_limit_bytes=56 * 2**20
        ),
    )(span_order, queries, keys, values, out_grad)
    return pl.pallas_call(
        last_columns,
        out_shape=(
            jax.ShapeDtypeStruct(queries.shape, BF16),
            jax.ShapeDtypeStruct(keys.shape, BF16),
            jax.ShapeDtypeStruct(values.shape, BF16),
        ),
    )(*parts)


def solution(mesh):
    rows = P(("head", "inner", "outer"), None)
    return jax.shard_map(
        body,
        mesh=mesh,
        in_specs=(rows, rows, rows, rows, P()),
        out_specs=(rows, rows, rows),
        check_vma=False,
    )
```

```python
import math

import jax
import jax.numpy as jnp
from jax import lax
from jax.experimental import pallas as pl
from jax.experimental.pallas import tpu as pltpu
from jax.sharding import PartitionSpec as P

MESH = pl.DeviceIdType.MESH
D = 128
G = 4
NY, NZ, NX, NC = 4, 8, 4, 2
U = 32
C = NY * U
QR = NX * C
KB = NC * C
GD = G * D
F32, BF16 = jnp.float32, jnp.bfloat16
SCALE = 1.0 / math.sqrt(D)
LOG2E = 1.4426950408889634
NT = (((1,), (1,)), ((), ()))
NN = (((1,), (0,)), ((), ()))
REL = (0, 1, 3, 2)


def dot(a, b, dims):
    return lax.dot_general(a, b, dims, preferred_element_type=F32)


def kernel(
    span, q_in, k_in, v_in, g_in, q_parts, kv_parts,
    qg, kv, kt, es, ds, qp, nsum, wsum, stat, stat_in, total, dqt, dkv, sib_in, z_out, z_in,
    dq_out, dq_in, q_fin, kv_fin,
    loc_sem, y_send, y_recv, x_send, x_recv, z_send, z_recv, c_send, c_recv,
    st_send, st_recv, dc_send, dc_recv, dz_send, dz_recv, dx_send, dx_recv, o_send, o_recv,
):
    y, zl, o = lax.axis_index("head"), lax.axis_index("inner"), lax.axis_index("outer")
    zh, x, c = o // (NX * NC), (o // NC) % NX, o % NC
    z = zh * 2 + zl

    def dev(y, z, x, c):
        return (y, z % 2, ((z // 2) * NX + x) * NC + c)

    def up(value, count, step):
        return (value + step + count) % count

    def copy(src, dst, send, recv, device):
        return pltpu.make_async_remote_copy(
            src_ref=src, dst_ref=dst, send_sem=send, recv_sem=recv, device_id=device, device_id_type=MESH
        )

    def y_dev(s):
        return dev(up(y, NY, s), z, x, c)

    def x_dev(s):
        return dev(y, z, up(x, NX, s), c)

    def z_dev(s):
        return dev(y, up(z, NZ, s), x, c)

    c_dev = dev(y, z, x, 1 - c)

    def away(p):
        return (p + 1) // 2 * (2 * (p % 2) - 1)

    def pieces(s):
        to, rows = up(y, NY, s), pl.ds((NY - s) % NY * U, U)
        wide = pl.ds(pl.multiple_of(to * GD, GD), GD)
        thin = pl.ds(pl.multiple_of(to * D, D), D)
        return (
            (k_in.at[:, thin], kv.at[rows, pl.ds(0, D)]),
            (v_in.at[:, thin], kv.at[rows, pl.ds(D, D)]),
            (q_in.at[:, wide], qg.at[rows, pl.ds(0, GD)]),
            (g_in.at[:, wide], qg.at[rows, pl.ds(GD, GD)]),
        )

    own = [pltpu.make_async_copy(a, b, loc_sem.at[i]) for i, (a, b) in enumerate(pieces(0))]
    for one in own:
        one.start()

    barrier = pltpu.get_barrier_semaphore()
    partners = (
        [y_dev(s) for s in range(1, NY)] + [x_dev(s) for s in range(1, NX)]
        + [z_dev(s) for s in (1, -1, 2, -2)] + [c_dev]
    )
    for device in partners:
        pl.semaphore_signal(barrier, inc=1, device_id=device, device_id_type=MESH)

    lane = lax.broadcasted_iota(jnp.int32, (8, QR), 1)
    places = jnp.zeros((8, QR), jnp.int32)
    for i in range(NX):
        for s in range(NY):
            unit = up(y, NY, s) * (NZ * NX * NC) + zl * (NZ // 2 * NX * NC) + (zh * NX + up(x, NX, REL[i])) * NC + c
            places = jnp.where(lane // U == i * NY + s, span[unit] * U, places)
    qp[...] = places + lane % U
    nsum[...] = jnp.zeros_like(nsum)
    wsum[...] = jnp.zeros_like(wsum)

    for one in own:
        one.wait()
    pl.semaphore_wait(barrier, len(partners))

    ys = {}
    for s in (1, 3, 2):
        for i, (a, b) in enumerate(pieces(s)):
            ys[s, i] = copy(a, b, y_send.at[s - 1, i], y_recv.at[s - 1, i], y_dev(s))
    def x_copy(way, s):
        rows = (NY - s) % NY * U
        slot, to, step, first, width = (
            (0, 2, 1, 0, 2 * GD), (0, 1, -1, 0, 2 * GD), (2, 3, 1, 0, GD), (1, 3, -1, GD, GD),
        )[way]
        return copy(
            qg.at[pl.ds(slot * C + rows, U), pl.ds(first, width)],
            qg.at[pl.ds(to * C + rows, U), pl.ds(first, width)],
            x_send.at[way, s], x_recv.at[way, s], x_dev(step),
        )

    def z_copy(i, slot, to, step, first, width):
        return copy(
            kv.at[pl.ds(slot * KB, C), pl.ds(first, width)],
            kv.at[pl.ds(to * KB, C), pl.ds(first, width)],
            z_send.at[i], z_recv.at[i], z_dev(step),
        )

    def c_copy(p):
        rows, there = p * KB, p * KB + C
        if not isinstance(p, int):
            rows, there = pl.multiple_of(rows, C), pl.multiple_of(there, C)
        return copy(kv.at[pl.ds(rows, C), :], kv.at[pl.ds(there, C), :], c_send.at[p], c_recv.at[p], c_dev)

    xs = {(way, s): x_copy(way, s) for way in range(4) for s in range(NY)}
    zs = {
        2: z_copy(2, 0, 2, 1, 0, 2 * D), 1: z_copy(1, 0, 1, -1, 0, 2 * D),
        4: z_copy(4, 0, 4, 2, 0, 2 * D), 3: z_copy(3, 0, 3, -2, 0, 2 * D),
        6: z_copy(6, 2, 6, 2, 0, 2 * D), 5: z_copy(5, 1, 5, -2, 0, 2 * D),
        7: z_copy(7, 4, 7, 2, 0, D), 8: z_copy(8, 3, 7, -2, D, D),
    }
    order = (0, 1, 3, 2)
    for i in range(2):
        for s in order[1:]:
            ys[s, i].start()
    xs[0, 0].start()
    xs[1, 0].start()
    for s in order[1:]:
        for i in (2, 3):
            ys[s, i].start()

    for s in order[1:]:
        ys[s, 0].wait_recv()
        ys[s, 1].wait_recv()
    for i in (2, 1, 4, 3):
        zs[i].start()
    c_copy(0).start()
    xs[0, 0].wait_recv()
    xs[2, 0].start()
    xs[1, 0].wait_recv()
    xs[3, 0].start()
    for s in order[1:]:
        ys[s, 2].wait_recv()
        ys[s, 3].wait_recv()
        xs[0, s].start()
        xs[1, s].start()
    for i in (2, 1):
        zs[i].wait_recv()
        zs[i + 4].start()
        c_copy(i).start()
    zs[4].wait_recv()
    zs[7].start()
    c_copy(4).start()
    zs[3].wait_recv()
    zs[8].start()
    c_copy(3).start()
    for s in order[1:]:
        xs[0, s].wait_recv()
        xs[2, s].start()
        xs[1, s].wait_recv()
        xs[3, s].start()

    row = lax.broadcasted_iota(jnp.int32, (U, 1), 0)

    def tile(p, count, low, width):
        rows = pl.ds(p * KB if isinstance(p, int) else pl.multiple_of(p * KB, KB), count * KB)
        keys, vals = kv[rows, 0:D], kv[rows, D : 2 * D]
        masks = []
        limit = jnp.broadcast_to(qp[0:1, low : low + width], (U, width))
        for i in range(count):
            zz = up(z, NZ, away(p + i))
            for cc in (c, 1 - c):
                for s in range(NY):
                    unit = up(y, NY, s) * (NZ * NX * NC) + (zz % 2) * (NZ // 2 * NX * NC) + ((zz // 2) * NX + x) * NC + cc
                    masks.append(row + span[unit] * U <= limit)
        mask = jnp.concatenate(masks, axis=0)
        for h in range(G):
            cols = slice(h * QR + low, h * QR + low + width)
            scores = dot(keys, qg[low : low + width, h * D : (h + 1) * D], NT)
            raised = jnp.where(mask, jnp.exp2(scores * (SCALE * LOG2E)), 0.0)
            grads = dot(vals, qg[low : low + width, GD + h * D : GD + (h + 1) * D], NT)
            es[rows, cols] = raised
            ds[rows, cols] = grads
            nsum[:, cols] += jnp.sum(raised.reshape(count * KB // 8, 8, width), axis=0)
            wsum[:, cols] += jnp.sum((raised * grads).reshape(count * KB // 8, 8, width), axis=0)

    def near(t, carry):
        @pl.when(t == 1)
        def _():
            for i in (6, 5):
                zs[i].wait_recv()
                c_copy(i).start()

        c_copy(2 * t).wait_recv()
        c_copy(2 * t + 1).wait_recv()
        tile(2 * t, 2, 0, QR // 2)
        return carry

    def far(t, carry):
        @pl.when(t == 1)
        def _():
            zs[7].wait_recv()
            zs[8].wait_recv()
            c_copy(7).start()

        tile(2 * t, 2, QR // 2, QR // 2)
        return carry

    lax.fori_loop(0, 3, near, 0)
    c_copy(6).wait_recv()
    tile(6, 1, 0, QR // 2)
    for s in range(NY):
        xs[2, s].wait_recv()
        xs[3, s].wait_recv()
    lax.fori_loop(0, 3, far, 0)
    c_copy(7).wait_recv()
    tile(6, 2, QR // 2, QR // 2)
    tile(7, 1, 0, QR // 2)

    for h in range(G):
        cols = slice(h * QR, (h + 1) * QR)
        stat[h : h + 1, :] = jnp.sum(nsum[:, cols], axis=0, keepdims=True)
        stat[G + h : G + h + 1, :] = jnp.sum(wsum[:, cols], axis=0, keepdims=True)
    stats = [
        copy(stat, stat_in.at[s - 1], st_send.at[s - 1], st_recv.at[s - 1], x_dev(s)) for s in range(1, NX)
    ]
    for one in stats:
        one.start()
    dqt[...] = jnp.zeros_like(dqt)
    for p in range(NZ):
        kt[:, p * KB : (p + 1) * KB] = kv[p * KB : (p + 1) * KB, 0:D].T
    for one in stats:
        one.wait_recv()
    for i in range(NX):
        both = stat[:, i * C : (i + 1) * C]
        for s in range(1, NX):
            j = REL.index((REL[i] + s) % NX)
            both += stat_in[s - 1, :, j * C : (j + 1) * C]
        inverse = 1.0 / both[0:G]
        total[0:G, i * C : (i + 1) * C] = inverse
        total[G : 2 * G, i * C : (i + 1) * C] = both[G : 2 * G] * inverse

    def half(p, core):
        return pl.ds(pl.multiple_of(p * KB + core * C, C), C)

    def to_sibling(p):
        return copy(dkv.at[half(p, 1), :], sib_in.at[p], dc_send.at[p], dc_recv.at[p], c_dev)

    def z_sum(i, p, step, first, width):
        cols = pl.ds(first, width)
        return copy(z_out.at[p, :, cols], z_in.at[p, :, cols], dz_send.at[i], dz_recv.at[i], z_dev(step))

    zsums = {
        7: z_sum(7, 7, 2, 0, D), 8: z_sum(8, 7, -2, D, D),
        6: z_sum(6, 6, -1, 0, 2 * D), 5: z_sum(5, 5, 1, 0, 2 * D),
        4: z_sum(4, 4, -2, 0, 2 * D), 3: z_sum(3, 3, 2, 0, 2 * D),
        2: z_sum(2, 2, -1, 0, 2 * D), 1: z_sum(1, 1, 1, 0, 2 * D),
    }

    def finish(p):
        to_sibling(p).wait_recv()
        z_out[p] = (dkv[half(p, 0), :] + sib_in[p]).astype(BF16)

    def relay(p, nearer, part, first):
        to_sibling(p).wait_recv()
        zsums[nearer].wait_recv()
        zsums[part].wait_recv()
        both = dkv[half(p, 0), :] + sib_in[p] + z_in[nearer].astype(F32)
        cols, rest = slice(first, first + D), slice(D - first, 2 * D - first)
        z_out[p, :, cols] = (both[:, cols] + z_in[7, :, cols].astype(F32)).astype(BF16)
        z_out[p, :, rest] = both[:, rest].astype(BF16)
        zsums[p].start()

    def sums(heads, rows):
        key_sum = jnp.zeros((2 * KB, D), F32)
        val_sum = jnp.zeros((2 * KB, D), F32)
        for h in heads:
            cols = slice(h * QR, (h + 1) * QR)
            weights = es[rows, cols] * total[h : h + 1, :]
            probs = weights.astype(BF16)
            slopes = (weights * (ds[rows, cols] - total[G + h : G + h + 1, :])).astype(BF16)
            val_sum += dot(probs, qg[:, GD + h * D : GD + (h + 1) * D], NN)
            key_sum += dot(slopes, qg[:, h * D : (h + 1) * D], NN)
            dqt[h] += dot(kt[:, rows], slopes, NN)
        return key_sum, val_sum

    def blocks(t):
        return pl.ds(pl.multiple_of((NZ - 2 - 2 * t) * KB, 2 * KB), 2 * KB)

    def second(t, carry):
        rows = blocks(t)
        dkv[rows, 0:D], dkv[rows, D : 2 * D] = sums(range(0, G // 2), rows)
        return carry

    def third(t, carry):
        rows = blocks(t)
        key_sum, val_sum = sums(range(G // 2, G), rows)
        dkv[rows, 0:D] += key_sum
        dkv[rows, D : 2 * D] += val_sum
        to_sibling(NZ - 1 - 2 * t).start()
        to_sibling(NZ - 2 - 2 * t).start()

        @pl.when(t == 1)
        def _():
            finish(7)
            zsums[7].start()
            zsums[8].start()
            finish(6)
            zsums[6].start()

        @pl.when(t == 2)
        def _():
            finish(5)
            zsums[5].start()

        @pl.when(t == 3)
        def _():
            finish(2)
            zsums[2].start()

        return carry

    def q_sums(half):
        cols = pl.ds(half * GD // 2, GD // 2)
        for h in range(half * G // 2, (half + 1) * G // 2):
            dq_out[:, h * D : (h + 1) * D] = (dqt[h].T * SCALE).astype(BF16)
        copies = []
        for s in (2, 1, 3):
            part = dq_out.at[pl.ds(REL.index(s) * C, C), cols]
            i = half * NX + s
            copies.append(copy(part, dq_in.at[s - 1, :, cols], dx_send.at[i], dx_recv.at[i], x_dev(s)))
        for one in copies:
            one.start()
        return copies

    def to_tokens(i, src, dst):
        copies = [pltpu.make_async_copy(src.at[pl.ds(0, U), :], dst, loc_sem.at[i])]
        for s in range(1, NY):
            copies.append(copy(src.at[pl.ds(s * U, U), :], dst, o_send.at[i, s], o_recv.at[i, s], y_dev(s)))
        for one in copies:
            one.start()
        return copies

    def q_done(half, copies):
        cols = slice(half * GD // 2, (half + 1) * GD // 2)
        for one in copies:
            one.wait_recv()
        q_sum = dq_out[0:C, cols].astype(F32)
        for s in range(1, NX):
            q_sum += dq_in[s - 1, :, cols].astype(F32)
        q_fin[half] = q_sum.astype(BF16)
        return to_tokens(half, q_fin.at[half], q_parts.at[y, half])

    lax.fori_loop(0, NZ // 2, second, 0)
    low_sums = q_sums(0)
    lax.fori_loop(0, NZ // 2, third, 0)
    high_sums = q_sums(1)
    finish(1)
    zsums[1].start()
    relay(4, 6, 8, D)
    relay(3, 5, 7, 0)
    outs = q_done(0, low_sums)
    to_sibling(0).wait_recv()
    kv_sum = dkv[0:C, :] + sib_in[0]
    for p in (1, 2):
        zsums[p].wait_recv()
        kv_sum += z_in[p].astype(F32)
    outs += q_done(1, high_sums)
    for p in (3, 4):
        zsums[p].wait_recv()
        kv_sum += z_in[p].astype(F32)
    kv_fin[:, 0:D] = (kv_sum[:, 0:D] * SCALE).astype(BF16)
    kv_fin[:, D : 2 * D] = kv_sum[:, D : 2 * D].astype(BF16)
    outs += to_tokens(2, kv_fin, kv_parts.at[y])

    for one in [*ys.values(), *xs.values(), *zs.values(), *zsums.values(), *stats, *low_sums, *high_sums]:
        one.wait_send()
    for p in range(NZ):
        c_copy(p).wait_send()
        to_sibling(p).wait_send()
    for one in outs:
        one.wait()


def last_columns(q_parts, kv_parts, q_out, k_out, v_out):
    for h in range(NY):
        for half in range(2):
            first = h * GD + half * GD // 2
            q_out[:, first : first + GD // 2] = q_parts[h, half]
        k_out[:, h * D : (h + 1) * D] = kv_parts[h, :, 0:D]
        v_out[:, h * D : (h + 1) * D] = kv_parts[h, :, D : 2 * D]


def body(queries, keys, values, out_grad, span_order):
    keys_all = NZ * NC * C
    dma = pltpu.SemaphoreType.DMA
    anywhere = pl.BlockSpec(memory_space=pl.ANY)
    parts = pl.pallas_call(
        kernel,
        out_shape=(
            jax.ShapeDtypeStruct((NY, 2, U, GD // 2), BF16),
            jax.ShapeDtypeStruct((NY, U, 2 * D), BF16),
        ),
        in_specs=[pl.BlockSpec(memory_space=pltpu.SMEM)] + [anywhere] * 4,
        out_specs=(anywhere,) * 2,
        scratch_shapes=[
            pltpu.VMEM((QR, 2 * GD), BF16),
            pltpu.VMEM((keys_all, 2 * D), BF16),
            pltpu.VMEM((D, keys_all), BF16),
            pltpu.VMEM((keys_all, G * QR), F32),
            pltpu.VMEM((keys_all, G * QR), F32),
            pltpu.VMEM((8, QR), jnp.int32),
            pltpu.VMEM((8, G * QR), F32),
            pltpu.VMEM((8, G * QR), F32),
            pltpu.VMEM((2 * G, QR), F32),
            pltpu.VMEM((NX - 1, 2 * G, QR), F32),
            pltpu.VMEM((2 * G, QR), F32),
            pltpu.VMEM((G, D, QR), F32),
            pltpu.VMEM((keys_all, 2 * D), F32),
            pltpu.VMEM((NZ, C, 2 * D), F32),
            pltpu.VMEM((NZ, C, 2 * D), BF16),
            pltpu.VMEM((NZ, C, 2 * D), BF16),
            pltpu.VMEM((QR, GD), BF16),
            pltpu.VMEM((NX - 1, C, GD), BF16),
            pltpu.VMEM((2, C, GD // 2), BF16),
            pltpu.VMEM((C, 2 * D), BF16),
            dma((4,)),
            dma((NY - 1, 4)), dma((NY - 1, 4)),
            dma((4, NY)), dma((4, NY)),
            dma((NZ + 1,)), dma((NZ + 1,)),
            dma((NZ,)), dma((NZ,)),
            dma((NX - 1,)), dma((NX - 1,)),
            dma((NZ,)), dma((NZ,)),
            dma((NZ + 1,)), dma((NZ + 1,)),
            dma((2 * NX,)), dma((2 * NX,)),
            dma((3, NY)), dma((3, NY)),
        ],
        compiler_params=pltpu.CompilerParams(
            collective_id=0, has_side_effects=True, vmem_limit_bytes=56 * 2**20
        ),
    )(span_order, queries, keys, values, out_grad)
    return pl.pallas_call(
        last_columns,
        out_shape=(
            jax.ShapeDtypeStruct(queries.shape, BF16),
            jax.ShapeDtypeStruct(keys.shape, BF16),
            jax.ShapeDtypeStruct(values.shape, BF16),
        ),
    )(*parts)


def solution(mesh):
    rows = P(("head", "inner", "outer"), None)
    return jax.shard_map(
        body,
        mesh=mesh,
        in_specs=(rows, rows, rows, rows, P()),
        out_specs=(rows, rows, rows),
        check_vma=False,
    )
```

```python
import math

import jax
import jax.numpy as jnp
from jax import lax
from jax.experimental import pallas as pl
from jax.experimental.pallas import tpu as pltpu
from jax.sharding import PartitionSpec as P

MESH = pl.DeviceIdType.MESH
D = 128
G = 4
NY, NZ, NX, NC = 4, 8, 4, 2
U = 32
C = NY * U
QR = NX * C
KB = NC * C
GD = G * D
F32, BF16 = jnp.float32, jnp.bfloat16
SCALE = 1.0 / math.sqrt(D)
LOG2E = 1.4426950408889634
NT = (((1,), (1,)), ((), ()))
NN = (((1,), (0,)), ((), ()))
REL = (0, 1, 3, 2)


def dot(a, b, dims):
    return lax.dot_general(a, b, dims, preferred_element_type=F32)


def kernel(
    span, q_in, k_in, v_in, g_in, q_parts, kv_parts,
    qg, kv, kt, es, ds, qp, nsum, wsum, stat, stat_in, total, dqt, dkv, sib_in, z_out, z_in,
    dq_out, dq_in, q_fin, kv_fin,
    loc_sem, y_send, y_recv, x_send, x_recv, z_send, z_recv, c_send, c_recv,
    st_send, st_recv, dc_send, dc_recv, dz_send, dz_recv, dx_send, dx_recv, o_send, o_recv,
):
    y, zl, o = lax.axis_index("head"), lax.axis_index("inner"), lax.axis_index("outer")
    zh, x, c = o // (NX * NC), (o // NC) % NX, o % NC
    z = zh * 2 + zl

    def dev(y, z, x, c):
        return (y, z % 2, ((z // 2) * NX + x) * NC + c)

    def up(value, count, step):
        return (value + step + count) % count

    def copy(src, dst, send, recv, device):
        return pltpu.make_async_remote_copy(
            src_ref=src, dst_ref=dst, send_sem=send, recv_sem=recv, device_id=device, device_id_type=MESH
        )

    def y_dev(s):
        return dev(up(y, NY, s), z, x, c)

    def x_dev(s):
        return dev(y, z, up(x, NX, s), c)

    def z_dev(s):
        return dev(y, up(z, NZ, s), x, c)

    c_dev = dev(y, z, x, 1 - c)

    def away(p):
        return (p + 1) // 2 * (2 * (p % 2) - 1)

    def pieces(s):
        to, rows = up(y, NY, s), pl.ds((NY - s) % NY * U, U)
        wide = pl.ds(pl.multiple_of(to * GD, GD), GD)
        thin = pl.ds(pl.multiple_of(to * D, D), D)
        return (
            (k_in.at[:, thin], kv.at[rows, pl.ds(0, D)]),
            (v_in.at[:, thin], kv.at[rows, pl.ds(D, D)]),
            (q_in.at[:, wide], qg.at[rows, pl.ds(0, GD)]),
            (g_in.at[:, wide], qg.at[rows, pl.ds(GD, GD)]),
        )

    own = [pltpu.make_async_copy(a, b, loc_sem.at[i]) for i, (a, b) in enumerate(pieces(0))]
    for one in own:
        one.start()

    barrier = pltpu.get_barrier_semaphore()
    partners = (
        [y_dev(s) for s in range(1, NY)] + [x_dev(s) for s in range(1, NX)]
        + [z_dev(s) for s in (1, -1, 2, -2)] + [c_dev]
    )
    for device in partners:
        pl.semaphore_signal(barrier, inc=1, device_id=device, device_id_type=MESH)

    lane = lax.broadcasted_iota(jnp.int32, (8, QR), 1)
    places = jnp.zeros((8, QR), jnp.int32)
    for i in range(NX):
        for s in range(NY):
            unit = up(y, NY, s) * (NZ * NX * NC) + zl * (NZ // 2 * NX * NC) + (zh * NX + up(x, NX, REL[i])) * NC + c
            places = jnp.where(lane // U == i * NY + s, span[unit] * U, places)
    qp[...] = places + lane % U
    nsum[...] = jnp.zeros_like(nsum)
    wsum[...] = jnp.zeros_like(wsum)

    for one in own:
        one.wait()
    pl.semaphore_wait(barrier, len(partners))

    ys = {}
    for s in (1, 3, 2):
        for i, (a, b) in enumerate(pieces(s)):
            ys[s, i] = copy(a, b, y_send.at[s - 1, i], y_recv.at[s - 1, i], y_dev(s))
    def x_copy(way, s):
        rows = (NY - s) % NY * U
        slot, to, step, first, width = (
            (0, 2, 1, 0, 2 * GD), (0, 1, -1, 0, 2 * GD), (2, 3, 1, 0, GD), (1, 3, -1, GD, GD),
        )[way]
        return copy(
            qg.at[pl.ds(slot * C + rows, U), pl.ds(first, width)],
            qg.at[pl.ds(to * C + rows, U), pl.ds(first, width)],
            x_send.at[way, s], x_recv.at[way, s], x_dev(step),
        )

    def z_copy(i, slot, to, step, first, width):
        return copy(
            kv.at[pl.ds(slot * KB, C), pl.ds(first, width)],
            kv.at[pl.ds(to * KB, C), pl.ds(first, width)],
            z_send.at[i], z_recv.at[i], z_dev(step),
        )

    def c_copy(p):
        rows, there = p * KB, p * KB + C
        if not isinstance(p, int):
            rows, there = pl.multiple_of(rows, C), pl.multiple_of(there, C)
        return copy(kv.at[pl.ds(rows, C), :], kv.at[pl.ds(there, C), :], c_send.at[p], c_recv.at[p], c_dev)

    xs = {(way, s): x_copy(way, s) for way in range(4) for s in range(NY)}
    zs = {
        2: z_copy(2, 0, 2, 1, 0, 2 * D), 1: z_copy(1, 0, 1, -1, 0, 2 * D),
        4: z_copy(4, 0, 4, 2, 0, 2 * D), 3: z_copy(3, 0, 3, -2, 0, 2 * D),
        6: z_copy(6, 2, 6, 2, 0, 2 * D), 5: z_copy(5, 1, 5, -2, 0, 2 * D),
        7: z_copy(7, 4, 7, 2, 0, D), 8: z_copy(8, 3, 7, -2, D, D),
    }
    order = (0, 1, 3, 2)
    for i in range(2):
        for s in order[1:]:
            ys[s, i].start()
    xs[0, 0].start()
    xs[1, 0].start()
    for s in order[1:]:
        for i in (2, 3):
            ys[s, i].start()

    for s in order[1:]:
        ys[s, 0].wait_recv()
        ys[s, 1].wait_recv()
    for i in (2, 1, 4, 3):
        zs[i].start()
    c_copy(0).start()
    xs[0, 0].wait_recv()
    xs[2, 0].start()
    xs[1, 0].wait_recv()
    xs[3, 0].start()
    for s in order[1:]:
        ys[s, 2].wait_recv()
        ys[s, 3].wait_recv()
        xs[0, s].start()
        xs[1, s].start()
    for i in (2, 1):
        zs[i].wait_recv()
        zs[i + 4].start()
        c_copy(i).start()
    zs[4].wait_recv()
    zs[7].start()
    c_copy(4).start()
    zs[3].wait_recv()
    zs[8].start()
    c_copy(3).start()
    for s in order[1:]:
        xs[0, s].wait_recv()
        xs[2, s].start()
        xs[1, s].wait_recv()
        xs[3, s].start()

    row = lax.broadcasted_iota(jnp.int32, (U, 1), 0)

    def tile(p, count, low, width):
        rows = pl.ds(p * KB if isinstance(p, int) else pl.multiple_of(p * KB, KB), count * KB)
        keys, vals = kv[rows, 0:D], kv[rows, D : 2 * D]
        masks = []
        limit = jnp.broadcast_to(qp[0:1, low : low + width], (U, width))
        for i in range(count):
            zz = up(z, NZ, away(p + i))
            for cc in (c, 1 - c):
                for s in range(NY):
                    unit = up(y, NY, s) * (NZ * NX * NC) + (zz % 2) * (NZ // 2 * NX * NC) + ((zz // 2) * NX + x) * NC + cc
                    masks.append(row + span[unit] * U <= limit)
        mask = jnp.concatenate(masks, axis=0)
        for h in range(G):
            cols = slice(h * QR + low, h * QR + low + width)
            scores = dot(keys, qg[low : low + width, h * D : (h + 1) * D], NT)
            raised = jnp.where(mask, jnp.exp2(scores * (SCALE * LOG2E)), 0.0)
            grads = dot(vals, qg[low : low + width, GD + h * D : GD + (h + 1) * D], NT)
            es[rows, cols] = raised
            ds[rows, cols] = grads
            nsum[:, cols] += jnp.sum(raised.reshape(count * KB // 8, 8, width), axis=0)
            wsum[:, cols] += jnp.sum((raised * grads).reshape(count * KB // 8, 8, width), axis=0)

    def near(t, carry):
        @pl.when(t == 1)
        def _():
            for i in (6, 5):
                zs[i].wait_recv()
                c_copy(i).start()

        c_copy(2 * t).wait_recv()
        c_copy(2 * t + 1).wait_recv()
        tile(2 * t, 2, 0, QR // 2)
        return carry

    def far(t, carry):
        @pl.when(t == 1)
        def _():
            zs[7].wait_recv()
            zs[8].wait_recv()
            c_copy(7).start()

        tile(2 * t, 2, QR // 2, QR // 2)
        return carry

    lax.fori_loop(0, 3, near, 0)
    c_copy(6).wait_recv()
    tile(6, 1, 0, QR // 2)
    for s in range(NY):
        xs[2, s].wait_recv()
        xs[3, s].wait_recv()
    lax.fori_loop(0, 3, far, 0)
    c_copy(7).wait_recv()
    tile(6, 2, QR // 2, QR // 2)
    tile(7, 1, 0, QR // 2)

    for h in range(G):
        cols = slice(h * QR, (h + 1) * QR)
        stat[h : h + 1, :] = jnp.sum(nsum[:, cols], axis=0, keepdims=True)
        stat[G + h : G + h + 1, :] = jnp.sum(wsum[:, cols], axis=0, keepdims=True)
    stats = [
        copy(stat, stat_in.at[s - 1], st_send.at[s - 1], st_recv.at[s - 1], x_dev(s)) for s in range(1, NX)
    ]
    for one in stats:
        one.start()
    dqt[...] = jnp.zeros_like(dqt)
    for p in range(NZ):
        kt[:, p * KB : (p + 1) * KB] = kv[p * KB : (p + 1) * KB, 0:D].T
    for one in stats:
        one.wait_recv()
    for i in range(NX):
        both = stat[:, i * C : (i + 1) * C]
        for s in range(1, NX):
            j = REL.index((REL[i] + s) % NX)
            both += stat_in[s - 1, :, j * C : (j + 1) * C]
        inverse = 1.0 / both[0:G]
        total[0:G, i * C : (i + 1) * C] = inverse
        total[G : 2 * G, i * C : (i + 1) * C] = both[G : 2 * G] * inverse

    def half(p, core):
        return pl.ds(pl.multiple_of(p * KB + core * C, C), C)

    def to_sibling(p):
        return copy(dkv.at[half(p, 1), :], sib_in.at[p], dc_send.at[p], dc_recv.at[p], c_dev)

    def z_sum(i, p, step, first, width):
        cols = pl.ds(first, width)
        return copy(z_out.at[p, :, cols], z_in.at[p, :, cols], dz_send.at[i], dz_recv.at[i], z_dev(step))

    zsums = {
        7: z_sum(7, 7, 2, 0, D), 8: z_sum(8, 7, -2, D, D),
        6: z_sum(6, 6, -1, 0, 2 * D), 5: z_sum(5, 5, 1, 0, 2 * D),
        4: z_sum(4, 4, -2, 0, 2 * D), 3: z_sum(3, 3, 2, 0, 2 * D),
        2: z_sum(2, 2, -1, 0, 2 * D), 1: z_sum(1, 1, 1, 0, 2 * D),
    }

    def finish(p):
        to_sibling(p).wait_recv()
        z_out[p] = (dkv[half(p, 0), :] + sib_in[p]).astype(BF16)

    def relay(p, nearer, part, first):
        to_sibling(p).wait_recv()
        zsums[nearer].wait_recv()
        zsums[part].wait_recv()
        both = dkv[half(p, 0), :] + sib_in[p] + z_in[nearer].astype(F32)
        cols, rest = slice(first, first + D), slice(D - first, 2 * D - first)
        z_out[p, :, cols] = (both[:, cols] + z_in[7, :, cols].astype(F32)).astype(BF16)
        z_out[p, :, rest] = both[:, rest].astype(BF16)
        zsums[p].start()

    def sums(heads, rows, count):
        key_sum = jnp.zeros((count * KB, D), F32)
        val_sum = jnp.zeros((count * KB, D), F32)
        for h in heads:
            cols = slice(h * QR, (h + 1) * QR)
            weights = es[rows, cols] * total[h : h + 1, :]
            probs = weights.astype(BF16)
            slopes = (weights * (ds[rows, cols] - total[G + h : G + h + 1, :])).astype(BF16)
            val_sum += dot(probs, qg[:, GD + h * D : GD + (h + 1) * D], NN)
            key_sum += dot(slopes, qg[:, h * D : (h + 1) * D], NN)
            dqt[h] += dot(kt[:, rows], slopes, NN)
        return key_sum, val_sum

    def blocks(t):
        return pl.ds(pl.multiple_of((NZ - 2 - 2 * t) * KB, 2 * KB), 2 * KB)

    def second(t, carry):
        rows = pl.ds(pl.multiple_of(t * 4 * KB, 4 * KB), 4 * KB)
        dkv[rows, 0:D], dkv[rows, D : 2 * D] = sums(range(0, G // 2), rows, 4)
        return carry

    def third(t, carry):
        rows = blocks(t)
        key_sum, val_sum = sums(range(G // 2, G), rows, 2)
        dkv[rows, 0:D] += key_sum
        dkv[rows, D : 2 * D] += val_sum
        to_sibling(NZ - 1 - 2 * t).start()
        to_sibling(NZ - 2 - 2 * t).start()

        @pl.when(t == 1)
        def _():
            finish(7)
            zsums[7].start()
            zsums[8].start()
            finish(6)
            zsums[6].start()

        @pl.when(t == 2)
        def _():
            finish(5)
            zsums[5].start()

        @pl.when(t == 3)
        def _():
            finish(2)
            zsums[2].start()

        return carry

    def q_sums(half):
        cols = pl.ds(half * GD // 2, GD // 2)
        for h in range(half * G // 2, (half + 1) * G // 2):
            dq_out[:, h * D : (h + 1) * D] = (dqt[h].T * SCALE).astype(BF16)
        copies = []
        for s in (2, 1, 3):
            part = dq_out.at[pl.ds(REL.index(s) * C, C), cols]
            i = half * NX + s
            copies.append(copy(part, dq_in.at[s - 1, :, cols], dx_send.at[i], dx_recv.at[i], x_dev(s)))
        for one in copies:
            one.start()
        return copies

    def to_tokens(i, src, dst):
        copies = [pltpu.make_async_copy(src.at[pl.ds(0, U), :], dst, loc_sem.at[i])]
        for s in range(1, NY):
            copies.append(copy(src.at[pl.ds(s * U, U), :], dst, o_send.at[i, s], o_recv.at[i, s], y_dev(s)))
        for one in copies:
            one.start()
        return copies

    def q_done(half, copies):
        cols = slice(half * GD // 2, (half + 1) * GD // 2)
        for one in copies:
            one.wait_recv()
        q_sum = dq_out[0:C, cols].astype(F32)
        for s in range(1, NX):
            q_sum += dq_in[s - 1, :, cols].astype(F32)
        q_fin[half] = q_sum.astype(BF16)
        return to_tokens(half, q_fin.at[half], q_parts.at[y, half])

    lax.fori_loop(0, NZ // 4, second, 0)
    low_sums = q_sums(0)
    lax.fori_loop(0, NZ // 2, third, 0)
    high_sums = q_sums(1)
    finish(1)
    zsums[1].start()
    relay(4, 6, 8, D)
    relay(3, 5, 7, 0)
    outs = q_done(0, low_sums)
    to_sibling(0).wait_recv()
    kv_sum = dkv[0:C, :] + sib_in[0]
    for p in (1, 2):
        zsums[p].wait_recv()
        kv_sum += z_in[p].astype(F32)
    outs += q_done(1, high_sums)
    for p in (3, 4):
        zsums[p].wait_recv()
        kv_sum += z_in[p].astype(F32)
    kv_fin[:, 0:D] = (kv_sum[:, 0:D] * SCALE).astype(BF16)
    kv_fin[:, D : 2 * D] = kv_sum[:, D : 2 * D].astype(BF16)
    outs += to_tokens(2, kv_fin, kv_parts.at[y])

    for one in [*ys.values(), *xs.values(), *zs.values(), *zsums.values(), *stats, *low_sums, *high_sums]:
        one.wait_send()
    for p in range(NZ):
        c_copy(p).wait_send()
        to_sibling(p).wait_send()
    for one in outs:
        one.wait()


def last_columns(q_parts, kv_parts, q_out, k_out, v_out):
    for h in range(NY):
        for half in range(2):
            first = h * GD + half * GD // 2
            q_out[:, first : first + GD // 2] = q_parts[h, half]
        k_out[:, h * D : (h + 1) * D] = kv_parts[h, :, 0:D]
        v_out[:, h * D : (h + 1) * D] = kv_parts[h, :, D : 2 * D]


def body(queries, keys, values, out_grad, span_order):
    keys_all = NZ * NC * C
    dma = pltpu.SemaphoreType.DMA
    anywhere = pl.BlockSpec(memory_space=pl.ANY)
    parts = pl.pallas_call(
        kernel,
        out_shape=(
            jax.ShapeDtypeStruct((NY, 2, U, GD // 2), BF16),
            jax.ShapeDtypeStruct((NY, U, 2 * D), BF16),
        ),
        in_specs=[pl.BlockSpec(memory_space=pltpu.SMEM)] + [anywhere] * 4,
        out_specs=(anywhere,) * 2,
        scratch_shapes=[
            pltpu.VMEM((QR, 2 * GD), BF16),
            pltpu.VMEM((keys_all, 2 * D), BF16),
            pltpu.VMEM((D, keys_all), BF16),
            pltpu.VMEM((keys_all, G * QR), F32),
            pltpu.VMEM((keys_all, G * QR), F32),
            pltpu.VMEM((8, QR), jnp.int32),
            pltpu.VMEM((8, G * QR), F32),
            pltpu.VMEM((8, G * QR), F32),
            pltpu.VMEM((2 * G, QR), F32),
            pltpu.VMEM((NX - 1, 2 * G, QR), F32),
            pltpu.VMEM((2 * G, QR), F32),
            pltpu.VMEM((G, D, QR), F32),
            pltpu.VMEM((keys_all, 2 * D), F32),
            pltpu.VMEM((NZ, C, 2 * D), F32),
            pltpu.VMEM((NZ, C, 2 * D), BF16),
            pltpu.VMEM((NZ, C, 2 * D), BF16),
            pltpu.VMEM((QR, GD), BF16),
            pltpu.VMEM((NX - 1, C, GD), BF16),
            pltpu.VMEM((2, C, GD // 2), BF16),
            pltpu.VMEM((C, 2 * D), BF16),
            dma((4,)),
            dma((NY - 1, 4)), dma((NY - 1, 4)),
            dma((4, NY)), dma((4, NY)),
            dma((NZ + 1,)), dma((NZ + 1,)),
            dma((NZ,)), dma((NZ,)),
            dma((NX - 1,)), dma((NX - 1,)),
            dma((NZ,)), dma((NZ,)),
            dma((NZ + 1,)), dma((NZ + 1,)),
            dma((2 * NX,)), dma((2 * NX,)),
            dma((3, NY)), dma((3, NY)),
        ],
        compiler_params=pltpu.CompilerParams(
            collective_id=0, has_side_effects=True, vmem_limit_bytes=56 * 2**20
        ),
    )(span_order, queries, keys, values, out_grad)
    return pl.pallas_call(
        last_columns,
        out_shape=(
            jax.ShapeDtypeStruct(queries.shape, BF16),
            jax.ShapeDtypeStruct(keys.shape, BF16),
            jax.ShapeDtypeStruct(values.shape, BF16),
        ),
    )(*parts)


def solution(mesh):
    rows = P(("head", "inner", "outer"), None)
    return jax.shard_map(
        body,
        mesh=mesh,
        in_specs=(rows, rows, rows, rows, P()),
        out_specs=(rows, rows, rows),
        check_vma=False,
    )
```
